256 devices in a mesh: freq: 4 (over x), tile: 64 (over y, z, core).
Axes of the slice: x: 4, y: 4, z: 8, core: 2. Of those that a mesh axis runs over, the one named last changes fastest.
Arguments:
- direct_field: float32 [16, 2, 64, 16384], P('freq', None, None, 'tile'), may hold values from -6 to 6
- u_factors: bfloat16 [16, 64, 64, 2, 16, 256], P('freq', 'tile'), may hold values from -0.1875 to 0.1875
- v_factors: bfloat16 [16, 64, 64, 2, 16, 256], P('freq', None, 'tile'), may hold values from -0.25 to 0.25
- tile_ranks: int32 [16, 64, 64], P('freq', 'tile'), may hold values from 1 to 16
- onsets_source: int32 [64, 16384], P(None, 'tile'), may hold values from 32 to 223
- onsets_receiver: int32 [64, 16384], P(None, 'tile'), may hold values from 32 to 223
Outputs:
- focus_plus: float32 [16, 2, 64, 16384], P('freq', None, None, 'tile')
- focus_minus: float32 [16, 2, 64, 16384], P('freq', None, None, 'tile')
The draws below stay inside these ranges and needn't reach their ends.
Inputs may be any that keep to these rules, and one draw needn't show every extreme that they name: Only the first tile_ranks rank rows of a tile's U and V belong to it.
All inputs are finite; a program needn't handle non-finite values.
Results may differ from the reference program's by a relative error of at most 0.0075.
Values may be sent and summed in bfloat16 or wider, within the bound.
No kernel may reach another device: no remote copies, remote signals or barrier semaphores. Data moves between devices by JAX's collectives and lax.ppermute only.
A program may use at most 128 MiB of HBM per device.

```python
import jax
import jax.numpy as jnp
from jax import lax

TILE = 256
RMAX = 16
FOCAL = 64
SAMPLES = 256
LOWBIN = 4
ITERS = 2
TILES = 64
GRID_COUNT = 16384
FREQS = 16


def place_ends(drawn, rng, smallest, largest):
    dims = drawn.shape
    index_at = [jax.random.randint(jax.random.fold_in(rng, axis), (), 0, dims[axis]) for axis in range(len(dims))]
    drawn = drawn.at[tuple(index_at)].set(smallest)
    longest = dims.index(max(dims))
    index_at[longest] = (index_at[longest] + 1) % dims[longest]
    return drawn.at[tuple(index_at)].set(largest)


def block_scale(own_key, shape, pieces, smallest, largest):
    gain = 1.0
    for position, shards_of in pieces:
        steps = jax.random.uniform(jax.random.fold_in(jax.random.fold_in(own_key, 6), position), (shards_of,), jnp.float32, smallest / len(pieces), largest / len(pieces))
        gain = gain * jnp.repeat(jnp.exp(steps), shape[position] // shards_of).reshape((-1,) + (1,) * (len(shape) - 1 - position))
    return gain


def scatter_about(key, shape, width, most, cuts=(), held_as=jnp.bfloat16):
    gain = block_scale(key, shape, cuts, -0.22, 0.18) if cuts else 1.0
    values = jax.random.normal(key, shape, jnp.float32) * width * gain
    return jnp.minimum(jnp.maximum(values, -most), most).astype(held_as)


def setup_inputs(seed: int = 0) -> dict:
    key_list = jax.random.split(jax.random.key(seed), 7)
    direct_field = scatter_about(key_list[0], (FREQS, 2, FOCAL, GRID_COUNT), 1.0, 6.0, ((0, 4), (3, 64)), jnp.float32)
    u_factors = scatter_about(key_list[1], (FREQS, TILES, TILES, 2, RMAX, TILE), (TILES * RMAX) ** -0.5, 0.1875, ((0, 4), (1, 64)))
    v_factors = scatter_about(key_list[2], (FREQS, TILES, TILES, 2, RMAX, TILE), (2 * TILE) ** -0.5, 0.25, ((0, 4), (2, 64)))
    tile_ranks = place_ends(jax.random.randint(key_list[3], (FREQS, TILES, TILES), 1, RMAX + 1), jax.random.fold_in(key_list[3], 1), 1, RMAX).astype(jnp.int32)
    onsets_source = place_ends(jax.random.randint(key_list[4], (FOCAL, GRID_COUNT), SAMPLES // 8, SAMPLES - SAMPLES // 8), jax.random.fold_in(key_list[4], 1), SAMPLES // 8, (SAMPLES - SAMPLES // 8) - 1).astype(jnp.int32)
    onsets_receiver = place_ends(jax.random.randint(key_list[5], (FOCAL, GRID_COUNT), SAMPLES // 8, SAMPLES - SAMPLES // 8), jax.random.fold_in(key_list[5], 1), SAMPLES // 8, (SAMPLES - SAMPLES // 8) - 1).astype(jnp.int32)
    return dict(direct_field=direct_field, u_factors=u_factors, v_factors=v_factors, tile_ranks=tile_ranks, onsets_source=onsets_source, onsets_receiver=onsets_receiver)


def band_tables(band_count, recording_duration, lowest):
    radian_rate = jnp.arange(band_count, dtype=jnp.int32) + lowest
    clock_moments = jnp.arange(recording_duration, dtype=jnp.int32)
    delay_rotations = (radian_rate[:, None] * clock_moments[None, :]) % recording_duration
    angles = (2.0 * jnp.pi / recording_duration) * delay_rotations.astype(jnp.float32)
    paired = jnp.stack([jnp.cos(angles), -jnp.sin(angles)], axis=1).reshape(2 * band_count, recording_duration)
    return paired.T, (2.0 / recording_duration) * paired


def rounded(values):
    return lax.optimization_barrier(values.astype(jnp.bfloat16)).astype(jnp.float32)


def rank_weights(ranks):
    return (jnp.arange(RMAX, dtype=jnp.int32) < ranks[..., None]).astype(jnp.float32)


def split_factors(u_block, v_block):
    return (u_block[:, :, 0].astype(jnp.float32), u_block[:, :, 1].astype(jnp.float32),
            v_block[:, :, 0].astype(jnp.float32), v_block[:, :, 1].astype(jnp.float32))


def forward_one(operands):
    u_block, v_block, ranks, field = operands
    u_real, u_imag, v_real, v_imag = split_factors(u_block, v_block)
    field_low = rounded(field).reshape(2, FOCAL, TILES, TILE)
    high = lax.Precision.HIGHEST
    form = "ijkn,pjn->ijkp"
    z_real = jnp.einsum(form, v_real, field_low[0], precision=high) + jnp.einsum(form, v_imag, field_low[1], precision=high)
    z_imag = jnp.einsum(form, v_real, field_low[1], precision=high) - jnp.einsum(form, v_imag, field_low[0], precision=high)
    weights = rank_weights(ranks)[..., None]
    z_real = rounded(z_real * weights)
    z_imag = rounded(z_imag * weights)
    back = "ijkn,ijkp->pin"
    y_real = jnp.einsum(back, u_real, z_real, precision=high) - jnp.einsum(back, u_imag, z_imag, precision=high)
    y_imag = jnp.einsum(back, u_real, z_imag, precision=high) + jnp.einsum(back, u_imag, z_real, precision=high)
    return jnp.stack([y_real, y_imag]).reshape(2, FOCAL, GRID_COUNT)


def adjoint_one(operands):
    u_block, v_block, ranks, field = operands
    u_real, u_imag, v_real, v_imag = split_factors(u_block, v_block)
    field_low = rounded(field).reshape(2, FOCAL, TILES, TILE)
    high = lax.Precision.HIGHEST
    form = "ijkn,pin->ijkp"
    w_real = jnp.einsum(form, u_real, field_low[0], precision=high) + jnp.einsum(form, u_imag, field_low[1], precision=high)
    w_imag = jnp.einsum(form, u_real, field_low[1], precision=high) - jnp.einsum(form, u_imag, field_low[0], precision=high)
    weights = rank_weights(ranks)[..., None]
    w_real = rounded(w_real * weights)
    w_imag = rounded(w_imag * weights)
    back = "ijkn,ijkp->pjn"
    x_real = jnp.einsum(back, v_real, w_real, precision=high) - jnp.einsum(back, v_imag, w_imag, precision=high)
    x_imag = jnp.einsum(back, v_real, w_imag, precision=high) + jnp.einsum(back, v_imag, w_real, precision=high)
    return jnp.stack([x_real, x_imag]).reshape(2, FOCAL, GRID_COUNT)


def window(spectra, onsets):
    inverse, forward = band_tables(FREQS, SAMPLES, LOWBIN)
    high = lax.Precision.HIGHEST
    blocks = spectra.reshape(2 * FREQS, FOCAL, TILES, TILE).transpose(2, 0, 1, 3).reshape(TILES, 2 * FREQS, FOCAL * TILE)
    limits = onsets.reshape(FOCAL, TILES, TILE).transpose(1, 0, 2).reshape(TILES, FOCAL * TILE)

    def window_mask_block(operands):
        block, limit = operands
        traces = jnp.dot(inverse, block, precision=high)
        inside = lax.broadcasted_iota(jnp.int32, traces.shape, 0) < limit[None, :]
        return jnp.dot(forward, jnp.where(inside, traces, 0.0), precision=high)

    result = lax.map(window_mask_block, (blocks, limits))
    return result.reshape(TILES, 2 * FREQS, FOCAL, TILE).transpose(1, 2, 0, 3).reshape(FREQS, 2, FOCAL, GRID_COUNT)


def reference(direct_field, u_factors, v_factors, tile_ranks, onsets_source, onsets_receiver):
    focus_plus = direct_field
    focus_minus = direct_field
    for iteration in range(ITERS):
        image = lax.map(forward_one, (u_factors, v_factors, tile_ranks, focus_plus))
        focus_minus = window(image, onsets_source)
        returned_field = lax.map(adjoint_one, (u_factors, v_factors, tile_ranks, focus_minus))
        focus_plus = direct_field + window(returned_field, onsets_receiver)
    return focus_plus, focus_minus
```

```python
import functools

import numpy as np
import jax
import jax.numpy as jnp
from jax import lax
from jax.experimental import pallas as pl
from jax.experimental.pallas import tpu as pltpu
from jax.sharding import PartitionSpec as P

TILE = 256
RMAX = 16
FOCAL = 64
SAMPLES = 256
LOWBIN = 4
ITERS = 2
TILES = 64
FREQS = 16
GROUPS = 4
OWN = FREQS // GROUPS
PW = 8
SETS = FOCAL // GROUPS // PW
VMEM_LIMIT = 48 * 1024 * 1024
BF = jnp.bfloat16
F32 = jnp.float32

FIELD = (OWN, SETS, 2 * PW, TILE)


def params():
    return pltpu.CompilerParams(vmem_limit_bytes=VMEM_LIMIT)


def dot_nt(a, b):
    return lax.dot_general(a, b, (((1,), (1,)), ((), ())), preferred_element_type=F32)


def dot_tn(a, b):
    return lax.dot_general(a, b, (((0,), (0,)), ((), ())), preferred_element_type=F32)


def focal_start(m, r, g):
    return pl.multiple_of(((m + GROUPS - r) % GROUPS * SETS + g) * PW, PW)


def project_kernel(forward, use_direct, use_field, *refs):
    refs = list(refs)
    o_ref = refs.pop()
    f_ref = refs.pop()
    if use_direct:
        m_ref, d_ref = refs[:2]
        refs = refs[2:]
    for f in range(OWN):
        plain, turned = [], []
        for r in range(GROUPS):
            for g in range(SETS):
                real = imag = None
                if use_direct:
                    at = pl.ds(focal_start(m_ref[0], r, g), PW)
                    real, imag = d_ref[f, 0, at, :], d_ref[f, 1, at, :]
                if use_field:
                    field = refs[r][f, g].astype(F32)
                    real = field[:PW] if real is None else real + field[:PW]
                    imag = field[PW:] if imag is None else imag + field[PW:]
                plain += [real, imag]
                turned += [imag, -real]
        total = None
        for part, rows in enumerate((plain, turned)):
            x = jnp.concatenate(rows, axis=0).astype(BF)
            factor = f_ref[f, :, 0, part] if forward else f_ref[f, 0, :, part]
            term = dot_nt(factor.reshape(TILES * RMAX, TILE), x)
            total = term if total is None else total + term
        o_ref[:, f] = total.astype(BF).reshape(TILES, RMAX, 2 * FOCAL)


def vmem(count=1):
    return [pl.BlockSpec(memory_space=pltpu.VMEM)] * count


def project(forward, factors, direct=None, me=None, field=None):
    ins, specs = [], []
    if direct is not None:
        ins += [me, direct]
        specs += [pl.BlockSpec(memory_space=pltpu.SMEM)] + vmem()
    if field is not None:
        ins += list(field)
        specs += vmem(GROUPS)
    return pl.pallas_call(
        functools.partial(project_kernel, forward, direct is not None, field is not None),
        in_specs=specs + vmem(),
        out_specs=vmem()[0],
        out_shape=jax.ShapeDtypeStruct((TILES, OWN, RMAX, 2 * FOCAL), BF),
        compiler_params=params(),
        cost_estimate=pl.CostEstimate(flops=600_000_000, bytes_accessed=5_000_000, transcendentals=0),
        name="project",
    )(*ins, factors)


def expand_kernel(forward, z_ref, f_ref, *outs):
    for f in range(OWN):
        z = z_ref[:, f].reshape(TILES * RMAX, 2 * FOCAL)
        straight, crossed = [
            dot_tn(z, (f_ref[f, 0, :, c] if forward else f_ref[f, :, 0, c]).reshape(TILES * RMAX, TILE))
            for c in range(2)
        ]
        for r in range(GROUPS):
            for g in range(SETS):
                at = (r * SETS + g) * 2 * PW
                real_part = straight[at : at + PW] - crossed[at + PW : at + 2 * PW]
                imag_part = straight[at + PW : at + 2 * PW] + crossed[at : at + PW]
                outs[-r % GROUPS][f, g] = jnp.concatenate([real_part, imag_part], axis=0).astype(BF)


def expand(forward, z, factors):
    return pl.pallas_call(
        functools.partial(expand_kernel, forward),
        in_specs=vmem(2),
        out_specs=vmem(GROUPS),
        out_shape=[jax.ShapeDtypeStruct(FIELD, BF)] * GROUPS,
        compiler_params=params(),
        cost_estimate=pl.CostEstimate(flops=600_000_000, bytes_accessed=5_000_000, transcendentals=0),
        name="expand",
    )(z, factors)


def window_kernel(s0, s1, s2, s3, onset_ref, t_ref, f_ref, *outs):
    rows = OWN * 2 * PW
    count = GROUPS * rows
    lane = lax.broadcasted_iota(jnp.int32, (1, count), 1) % PW
    row = lax.broadcasted_iota(jnp.int32, (count, 1), 0) % PW
    moment = lax.broadcasted_iota(jnp.int32, (SAMPLES, TILE), 0)
    fields = [
        jnp.concatenate([ref[:, g].reshape(rows, TILE) for ref in (s0, s1, s2, s3)], axis=0)
        for g in range(SETS)
    ]
    totals = [jnp.zeros((count, TILE), F32) for _ in range(SETS)]
    for p in range(PW):
        pick_lane = (lane == p).astype(F32).astype(BF)
        pick_row = (row == p).astype(F32).astype(BF)
        inverse = [t_ref[part] * pick_lane for part in range(2)]
        forward = [f_ref[part] * pick_row for part in range(2)]
        for g in range(SETS):
            trace = sum(jnp.dot(part, fields[g], preferred_element_type=F32) for part in inverse)
            limit = onset_ref[g * PW + p : g * PW + p + 1, :]
            kept = jnp.where(moment < limit, trace, 0.0).astype(BF)
            totals[g] += sum(jnp.dot(part, kept, preferred_element_type=F32) for part in forward)
    for g in range(SETS):
        result = totals[g].astype(BF)
        for r in range(GROUPS):
            outs[-r % GROUPS][:, g] = result[r * rows : (r + 1) * rows].reshape(OWN, 2 * PW, TILE)


def window(field, onset, tables):
    return pl.pallas_call(
        window_kernel,
        in_specs=vmem(GROUPS + 3),
        out_specs=vmem(GROUPS),
        out_shape=[jax.ShapeDtypeStruct(FIELD, BF)] * GROUPS,
        compiler_params=params(),
        cost_estimate=pl.CostEstimate(flops=2_200_000_000, bytes_accessed=1_000_000, transcendentals=0),
        name="window",
    )(*field, onset, *tables)


def finish_kernel(use_direct, *refs):
    refs = list(refs)
    o_ref = refs.pop()
    m_ref = refs.pop(0)
    d_ref = refs.pop(0) if use_direct else None
    for r in range(GROUPS):
        for g in range(SETS):
            at = pl.ds(focal_start(m_ref[0], r, g), PW)
            for f in range(OWN):
                field = refs[r][f, g].astype(F32)
                for c in range(2):
                    value = field[c * PW : (c + 1) * PW]
                    if use_direct:
                        value = value + d_ref[f, c, at, :]
                    o_ref[f, c, at, :] = value


def finish(me, field, direct=None):
    use_direct = direct is not None
    return pl.pallas_call(
        functools.partial(finish_kernel, use_direct),
        in_specs=[pl.BlockSpec(memory_space=pltpu.SMEM)] + vmem(use_direct + GROUPS),
        out_specs=vmem()[0],
        out_shape=jax.ShapeDtypeStruct((OWN, 2, FOCAL, TILE), F32),
        compiler_params=params(),
        cost_estimate=pl.CostEstimate(flops=1_000_000, bytes_accessed=1_000_000, transcendentals=0),
        name="finish",
    )(me, *([direct] if use_direct else []), *field)


def split_bf16(table):
    high = table.astype(jnp.bfloat16.dtype)
    return np.stack([high, (table - high.astype(np.float64)).astype(jnp.bfloat16.dtype)])


def table_constants():
    turns = (np.arange(FREQS)[:, None] + LOWBIN) * np.arange(SAMPLES)[None, :] % SAMPLES
    angles = 2.0 * np.pi / SAMPLES * turns
    paired = np.stack([np.cos(angles), -np.sin(angles)], axis=1)
    spread = np.repeat(paired.reshape(GROUPS, OWN, 2, 1, SAMPLES), PW, axis=3)
    order = [3, 2, 1, 0, 3, 2, 1]
    rows = spread[order].reshape(len(order) * OWN * 2 * PW, SAMPLES)
    return split_bf16(np.ascontiguousarray(rows.T)), split_bf16(2.0 / SAMPLES * rows)


def own_tables(me):
    inverse, forward = table_constants()
    count = FREQS * 2 * PW
    start = (GROUPS - 1 - me) * (OWN * 2 * PW)
    return (
        lax.dynamic_slice_in_dim(jnp.asarray(inverse), start, count, 2),
        lax.dynamic_slice_in_dim(jnp.asarray(forward), start, count, 1),
    )


def exchange(parts):
    steps = [
        lax.ppermute(parts[r], "freq", [(i, (i + r) % GROUPS) for i in range(GROUPS)])
        for r in range(1, GROUPS)
    ]
    return [parts[0]] + steps


def own_onsets(onsets, me):
    return lax.dynamic_slice_in_dim(onsets, me * (SETS * PW), SETS * PW, 0)


def route(z):
    return lax.all_to_all(
        z.reshape(TILES, OWN * RMAX, 2 * FOCAL), "tile", 0, 0, tiled=True
    ).reshape(z.shape)


def per_device(direct_field, u_factors, v_factors, tile_ranks, onsets_source, onsets_receiver):
    me = lax.axis_index("freq")
    index = me.reshape(1).astype(jnp.int32)
    tables = own_tables(me)
    sources, receivers = own_onsets(onsets_source, me), own_onsets(onsets_receiver, me)
    inside = lax.broadcasted_iota(jnp.int32, (1, 1, 1, 1, RMAX, 1), 4)
    u_own = u_factors * (inside < tile_ranks[:, :, :, None, None, None]).astype(BF)

    plus = None
    for _ in range(ITERS):
        z = project(True, v_factors, direct_field, index, plus)
        image = exchange(expand(True, route(z), u_own))
        minus = exchange(window(image, sources, tables))
        w = project(False, u_own, field=minus)
        image = exchange(expand(False, route(w), v_factors))
        plus = exchange(window(image, receivers, tables))
    return (finish(index, plus, direct_field), finish(index, minus))


def solution(mesh):
    return jax.shard_map(
        per_device,
        mesh=mesh,
        in_specs=(
            P("freq", None, None, "tile"),
            P("freq", "tile", None, None, None, None),
            P("freq", None, "tile", None, None, None),
            P("freq", "tile", None),
            P(None, "tile"),
            P(None, "tile"),
        ),
        out_specs=(P("freq", None, None, "tile"), P("freq", None, None, "tile")),
        check_vma=False,
    )
```

```python
import functools

import numpy as np
import jax
import jax.numpy as jnp
from jax import lax
from jax.experimental import pallas as pl
from jax.experimental.pallas import tpu as pltpu
from jax.sharding import PartitionSpec as P

TILE = 256
RMAX = 16
FOCAL = 64
SAMPLES = 256
LOWBIN = 4
ITERS = 2
TILES = 64
FREQS = 16
GROUPS = 4
OWN = FREQS // GROUPS
PW = 8
SETS = FOCAL // GROUPS // PW
VMEM_LIMIT = 24 * 1024 * 1024
BF = jnp.bfloat16
F32 = jnp.float32

FIELD = (OWN, SETS, 2 * PW, TILE)


def params():
    return pltpu.CompilerParams(vmem_limit_bytes=VMEM_LIMIT)


def dot_nt(a, b):
    return lax.dot_general(a, b, (((1,), (1,)), ((), ())), preferred_element_type=F32)


def dot_tn(a, b):
    return lax.dot_general(a, b, (((0,), (0,)), ((), ())), preferred_element_type=F32)


def focal_start(m, r, g):
    return pl.multiple_of(((m + GROUPS - r) % GROUPS * SETS + g) * PW, PW)


def project_kernel(forward, use_field, m_ref, *refs):
    refs = list(refs)
    o_ref = refs.pop()
    d_ref = refs.pop(0) if forward else None
    f_ref = refs.pop(0)
    for f in range(OWN):
        plain, turned = [], []
        for r in range(GROUPS):
            for g in range(SETS):
                real = imag = None
                if forward:
                    at = pl.ds(focal_start(m_ref[0], r, g), PW)
                    real, imag = d_ref[f, 0, at, :], d_ref[f, 1, at, :]
                if use_field:
                    field = refs[r][f, g].astype(F32)
                    real = field[:PW] if real is None else real + field[:PW]
                    imag = field[PW:] if imag is None else imag + field[PW:]
                plain += [real, imag]
                turned += [imag, -real]
        total = None
        for part, rows in enumerate((plain, turned)):
            x = jnp.concatenate(rows, axis=0).astype(BF)
            factor = f_ref[f, :, 0, part] if forward else f_ref[f, 0, :, part]
            term = dot_nt(factor.reshape(TILES * RMAX, TILE), x)
            total = term if total is None else total + term
        o_ref[:, f] = total.astype(BF).reshape(TILES, RMAX, 2 * FOCAL)


def vmem(count=1):
    return [pl.BlockSpec(memory_space=pltpu.VMEM)] * count


def project(me, factors, field=(), direct=None):
    forward = direct is not None
    ins = ([direct] if forward else []) + [factors] + list(field)
    return pl.pallas_call(
        functools.partial(project_kernel, forward, len(field) > 0),
        in_specs=[pl.BlockSpec(memory_space=pltpu.SMEM)] + vmem(len(ins)),
        out_specs=vmem()[0],
        out_shape=jax.ShapeDtypeStruct((TILES, OWN, RMAX, 2 * FOCAL), BF),
        compiler_params=params(),
        cost_estimate=pl.CostEstimate(flops=600_000_000, bytes_accessed=5_000_000, transcendentals=0),
        name="project",
    )(me, *ins)


def mask_kernel(mask_ref, f_ref, o_ref):
    for f in range(OWN):
        mask = jnp.concatenate([mask_ref[:, f]] * (TILE // 128), axis=2)
        for c in range(2):
            o_ref[f, 0, :, c] = f_ref[f, 0, :, c] * mask


def masked(factors, tile_ranks):
    rank = tile_ranks.transpose(2, 0, 1)
    mask = (lax.broadcasted_iota(jnp.int32, (1, 1, RMAX, 128), 2) < rank[..., None]).astype(BF)
    return pl.pallas_call(
        mask_kernel,
        in_specs=vmem(2),
        out_specs=vmem()[0],
        out_shape=jax.ShapeDtypeStruct(factors.shape, BF),
        compiler_params=params(),
        cost_estimate=pl.CostEstimate(flops=2_000_000, bytes_accessed=9_000_000, transcendentals=0),
        name="masked",
    )(mask, factors)


def expand_kernel(forward, z_ref, f_ref, *outs):
    for f in range(OWN):
        z = z_ref[:, f].reshape(TILES * RMAX, 2 * FOCAL)
        straight, crossed = [
            dot_tn(z, (f_ref[f, 0, :, c] if forward else f_ref[f, :, 0, c]).reshape(TILES * RMAX, TILE))
            for c in range(2)
        ]
        for r in range(GROUPS):
            for g in range(SETS):
                at = (r * SETS + g) * 2 * PW
                real_part = straight[at : at + PW] - crossed[at + PW : at + 2 * PW]
                imag_part = straight[at + PW : at + 2 * PW] + crossed[at : at + PW]
                outs[-r % GROUPS][f, g] = jnp.concatenate([real_part, imag_part], axis=0).astype(BF)


def expand(forward, z, factors):
    return pl.pallas_call(
        functools.partial(expand_kernel, forward),
        in_specs=vmem(2),
        out_specs=vmem(GROUPS),
        out_shape=[jax.ShapeDtypeStruct(FIELD, BF)] * GROUPS,
        compiler_params=params(),
        cost_estimate=pl.CostEstimate(flops=600_000_000, bytes_accessed=5_000_000, transcendentals=0),
        name="expand",
    )(z, factors)


def window_kernel(s0, s1, s2, s3, onset_ref, t_ref, f_ref, *outs):
    half = PW // 2
    rows = OWN * 2 * PW
    count = GROUPS * rows
    lane = lax.broadcasted_iota(jnp.int32, (1, count), 1) % PW
    row = lax.broadcasted_iota(jnp.int32, (count, 1), 0) % PW
    first = lax.broadcasted_iota(jnp.int32, (count, TILE), 0) % PW < half
    moment = lax.broadcasted_iota(jnp.int32, (SAMPLES, TILE), 0)

    def one(flags):
        return flags.astype(F32).astype(BF)

    inverse, forward = [], []
    for part in range(2):
        points = [(p, (p + half) % PW) for p in range(part * half, (part + 1) * half)]
        inverse.append(
            jnp.concatenate([t_ref[0] * one(lane == p) + t_ref[1] * one(lane == o) for p, o in points], axis=0)
        )
        forward.append(
            jnp.concatenate([f_ref[0] * one(row == p) + f_ref[1] * one(row == o) for p, o in points], axis=1)
        )
    for g in range(SETS):
        whole = jnp.concatenate(
            [ref[:, g].reshape(rows, TILE) for ref in (s0, s1, s2, s3)], axis=0
        ).astype(F32)
        down = pltpu.roll(whole, half, 0)
        up = pltpu.roll(whole, count - half, 0)
        fields = [jnp.where(first, whole, down).astype(BF), jnp.where(first, up, whole).astype(BF)]
        totals = []
        for part in range(2):
            trace = jnp.dot(inverse[part], fields[part], preferred_element_type=F32)
            kept = []
            for p in range(half):
                at = g * PW + part * half + p
                piece = trace[p * SAMPLES : (p + 1) * SAMPLES]
                kept.append(jnp.where(moment < onset_ref[at : at + 1, :], piece, 0.0).astype(BF))
            totals.append(
                jnp.dot(forward[part], jnp.concatenate(kept, axis=0), preferred_element_type=F32)
            )
        early, late = totals
        result = jnp.where(
            first, early + pltpu.roll(early, count - half, 0), late + pltpu.roll(late, half, 0)
        ).astype(BF)
        for r in range(GROUPS):
            outs[-r % GROUPS][:, g] = result[r * rows : (r + 1) * rows].reshape(OWN, 2 * PW, TILE)


def window(field, onset, tables):
    return pl.pallas_call(
        window_kernel,
        in_specs=vmem(GROUPS + 3),
        out_specs=vmem(GROUPS),
        out_shape=[jax.ShapeDtypeStruct(FIELD, BF)] * GROUPS,
        compiler_params=params(),
        cost_estimate=pl.CostEstimate(flops=1_100_000_000, bytes_accessed=1_000_000, transcendentals=0),
        name="window",
    )(*field, onset, *tables)


def finish_kernel(use_direct, *refs):
    refs = list(refs)
    o_ref = refs.pop()
    m_ref = refs.pop(0)
    d_ref = refs.pop(0) if use_direct else None
    for r in range(GROUPS):
        for g in range(SETS):
            at = pl.ds(focal_start(m_ref[0], r, g), PW)
            for f in range(OWN):
                field = refs[r][f, g].astype(F32)
                for c in range(2):
                    value = field[c * PW : (c + 1) * PW]
                    if use_direct:
                        value = value + d_ref[f, c, at, :]
                    o_ref[f, c, at, :] = value


def finish(me, field, direct=None):
    use_direct = direct is not None
    return pl.pallas_call(
        functools.partial(finish_kernel, use_direct),
        in_specs=[pl.BlockSpec(memory_space=pltpu.SMEM)] + vmem(use_direct + GROUPS),
        out_specs=vmem()[0],
        out_shape=jax.ShapeDtypeStruct((OWN, 2, FOCAL, TILE), F32),
        compiler_params=params(),
        cost_estimate=pl.CostEstimate(flops=1_000_000, bytes_accessed=1_000_000, transcendentals=0),
        name="finish",
    )(me, *([direct] if use_direct else []), *field)


def split_bf16(table):
    high = table.astype(jnp.bfloat16.dtype)
    return np.stack([high, (table - high.astype(np.float64)).astype(jnp.bfloat16.dtype)])


def table_constants():
    turns = (np.arange(FREQS)[:, None] + LOWBIN) * np.arange(SAMPLES)[None, :] % SAMPLES
    angles = 2.0 * np.pi / SAMPLES * turns
    paired = np.stack([np.cos(angles), -np.sin(angles)], axis=1)
    spread = np.repeat(paired.reshape(GROUPS, OWN, 2, 1, SAMPLES), PW, axis=3)
    order = [3, 2, 1, 0, 3, 2, 1]
    rows = spread[order].reshape(len(order) * OWN * 2 * PW, SAMPLES)
    return split_bf16(np.ascontiguousarray(rows.T)), split_bf16(2.0 / SAMPLES * rows)


def own_tables(me):
    inverse, forward = table_constants()
    count = FREQS * 2 * PW
    start = (GROUPS - 1 - me) * (OWN * 2 * PW)
    return (
        lax.dynamic_slice_in_dim(jnp.asarray(inverse), start, count, 2),
        lax.dynamic_slice_in_dim(jnp.asarray(forward), start, count, 1),
    )


def exchange(parts):
    steps = [
        lax.ppermute(parts[r], "freq", [(i, (i + r) % GROUPS) for i in range(GROUPS)])
        for r in range(1, GROUPS)
    ]
    return [parts[0]] + steps


def own_onsets(onsets, me):
    return lax.dynamic_slice_in_dim(onsets, me * (SETS * PW), SETS * PW, 0)


def route(z):
    return lax.all_to_all(
        z.reshape(TILES, OWN * RMAX, 2 * FOCAL), "tile", 0, 0, tiled=True
    ).reshape(z.shape)


def per_device(direct_field, u_factors, v_factors, tile_ranks, onsets_source, onsets_receiver):
    me = lax.axis_index("freq")
    index = me.reshape(1).astype(jnp.int32)
    tables = own_tables(me)
    sources, receivers = own_onsets(onsets_source, me), own_onsets(onsets_receiver, me)
    u_own = masked(u_factors, tile_ranks)

    plus = ()
    for _ in range(ITERS):
        z = project(index, v_factors, plus, direct_field)
        image = exchange(expand(True, route(z), u_own))
        minus = exchange(window(image, sources, tables))
        w = project(index, u_own, minus)
        image = exchange(expand(False, route(w), v_factors))
        plus = exchange(window(image, receivers, tables))
    return (finish(index, plus, direct_field), finish(index, minus))


def solution(mesh):
    return jax.shard_map(
        per_device,
        mesh=mesh,
        in_specs=(
            P("freq", None, None, "tile"),
            P("freq", "tile", None, None, None, None),
            P("freq", None, "tile", None, None, None),
            P("freq", "tile", None),
            P(None, "tile"),
            P(None, "tile"),
        ),
        out_specs=(P("freq", None, None, "tile"), P("freq", None, None, "tile")),
        check_vma=False,
    )
```

```python
import functools

import numpy as np
import jax
import jax.numpy as jnp
from jax import lax
from jax.experimental import pallas as pl
from jax.experimental.pallas import tpu as pltpu
from jax.sharding import PartitionSpec as P

TILE = 256
RMAX = 16
FOCAL = 64
SAMPLES = 256
LOWBIN = 4
ITERS = 2
TILES = 64
FREQS = 16
GROUPS = 4
OWN = FREQS // GROUPS
PW = 8
SETS = FOCAL // GROUPS // PW
VMEM_LIMIT = 24 * 1024 * 1024
BF = jnp.bfloat16
F32 = jnp.float32

FIELD = (OWN, SETS, 2 * PW, TILE)


def params():
    return pltpu.CompilerParams(vmem_limit_bytes=VMEM_LIMIT)


def dot_nt(a, b):
    return lax.dot_general(a, b, (((1,), (1,)), ((), ())), preferred_element_type=F32)


def dot_tn(a, b):
    return lax.dot_general(a, b, (((0,), (0,)), ((), ())), preferred_element_type=F32)


def focal_start(m, r, g):
    return pl.multiple_of(((m + GROUPS - r) % GROUPS * SETS + g) * PW, PW)


def project_kernel(forward, use_field, m_ref, *refs):
    d_ref, f_ref, *refs, o_ref = refs
    for f in range(OWN):
        plain, turned = [], []
        for r in range(GROUPS):
            for g in range(SETS):
                real = imag = None
                if forward:
                    at = pl.ds(focal_start(m_ref[0], r, g), PW)
                    real, imag = d_ref[f, 0, at, :], d_ref[f, 1, at, :]
                if use_field:
                    field = refs[r][f, g].astype(F32)
                    real = field[:PW] if real is None else real + field[:PW]
                    imag = field[PW:] if imag is None else imag + field[PW:]
                plain += [real, imag]
                turned += [imag, -real]
        total = None
        for part, rows in enumerate((plain, turned)):
            x = jnp.concatenate(rows, axis=0).astype(BF)
            factor = f_ref[f, :, 0, part] if forward else f_ref[f, 0, :, part]
            term = dot_nt(factor.reshape(TILES * RMAX, TILE), x)
            total = term if total is None else total + term
        z = total.astype(BF).reshape(TILES, RMAX, 2 * FOCAL)
        o_ref[:, f] = z if forward else z * d_ref[f]


def vmem(count=1):
    return [pl.BlockSpec(memory_space=pltpu.VMEM)] * count


def project(forward, me, other, factors, field=()):
    return pl.pallas_call(
        functools.partial(project_kernel, forward, len(field) > 0),
        in_specs=[pl.BlockSpec(memory_space=pltpu.SMEM)] + vmem(2 + len(field)),
        out_specs=vmem()[0],
        out_shape=jax.ShapeDtypeStruct((TILES, OWN, RMAX, 2 * FOCAL), BF),
        compiler_params=params(),
        cost_estimate=pl.CostEstimate(flops=600_000_000, bytes_accessed=5_000_000, transcendentals=0),
        name="project",
    )(me, other, factors, *field)


def expand_kernel(forward, z_ref, f_ref, *outs):
    if forward:
        mask_ref, *outs = outs
    for f in range(OWN):
        z = z_ref[:, f] * mask_ref[f] if forward else z_ref[:, f]
        z = z.reshape(TILES * RMAX, 2 * FOCAL)
        straight, crossed = [
            dot_tn(z, (f_ref[f, 0, :, c] if forward else f_ref[f, :, 0, c]).reshape(TILES * RMAX, TILE))
            for c in range(2)
        ]
        for r in range(GROUPS):
            for g in range(SETS):
                at = (r * SETS + g) * 2 * PW
                real_part = straight[at : at + PW] - crossed[at + PW : at + 2 * PW]
                imag_part = straight[at + PW : at + 2 * PW] + crossed[at : at + PW]
                outs[-r % GROUPS][f, g] = jnp.concatenate([real_part, imag_part], axis=0).astype(BF)


def expand(forward, z, factors, mask=None):
    ins = [z, factors] + ([mask] if forward else [])
    return pl.pallas_call(
        functools.partial(expand_kernel, forward),
        in_specs=vmem(len(ins)),
        out_specs=vmem(GROUPS),
        out_shape=[jax.ShapeDtypeStruct(FIELD, BF)] * GROUPS,
        compiler_params=params(),
        cost_estimate=pl.CostEstimate(flops=600_000_000, bytes_accessed=5_000_000, transcendentals=0),
        name="expand",
    )(*ins)


def window_kernel(s0, s1, s2, s3, onset_ref, t_ref, f_ref, *outs):
    half = PW // 2
    rows = OWN * 2 * PW
    count = GROUPS * rows
    lane = lax.broadcasted_iota(jnp.int32, (1, count), 1) % PW
    row = lax.broadcasted_iota(jnp.int32, (count, 1), 0) % PW
    first = lax.broadcasted_iota(jnp.int32, (count, TILE), 0) % PW < half
    moment = lax.broadcasted_iota(jnp.int32, (SAMPLES, TILE), 0)

    def one(flags):
        return flags.astype(F32).astype(BF)

    inverse, forward = [], []
    for part in range(2):
        points = [(p, (p + half) % PW) for p in range(part * half, (part + 1) * half)]
        inverse.append(
            jnp.concatenate([t_ref[0] * one(lane == p) + t_ref[1] * one(lane == o) for p, o in points], axis=0)
        )
        forward.append(
            jnp.concatenate([f_ref[0] * one(row == p) + f_ref[1] * one(row == o) for p, o in points], axis=1)
        )
    for g in range(SETS):
        whole = jnp.concatenate(
            [ref[:, g].reshape(rows, TILE) for ref in (s0, s1, s2, s3)], axis=0
        ).astype(F32)
        down = pltpu.roll(whole, half, 0)
        up = pltpu.roll(whole, count - half, 0)
        fields = [jnp.where(first, whole, down).astype(BF), jnp.where(first, up, whole).astype(BF)]
        totals = []
        for part in range(2):
            trace = jnp.dot(inverse[part], fields[part], preferred_element_type=F32)
            kept = []
            for p in range(half):
                at = g * PW + part * half + p
                piece = trace[p * SAMPLES : (p + 1) * SAMPLES]
                kept.append(jnp.where(moment < onset_ref[at : at + 1, :], piece, 0.0).astype(BF))
            totals.append(
                jnp.dot(forward[part], jnp.concatenate(kept, axis=0), preferred_element_type=F32)
            )
        early, late = totals
        result = jnp.where(
            first, early + pltpu.roll(early, count - half, 0), late + pltpu.roll(late, half, 0)
        ).astype(BF)
        for r in range(GROUPS):
            outs[-r % GROUPS][:, g] = result[r * rows : (r + 1) * rows].reshape(OWN, 2 * PW, TILE)


def window(field, onset, tables):
    return pl.pallas_call(
        window_kernel,
        in_specs=vmem(GROUPS + 3),
        out_specs=vmem(GROUPS),
        out_shape=[jax.ShapeDtypeStruct(FIELD, BF)] * GROUPS,
        compiler_params=params(),
        cost_estimate=pl.CostEstimate(flops=1_100_000_000, bytes_accessed=1_000_000, transcendentals=0),
        name="window",
    )(*field, onset, *tables)


def finish_kernel(use_direct, *refs):
    refs = list(refs)
    o_ref = refs.pop()
    m_ref = refs.pop(0)
    d_ref = refs.pop(0) if use_direct else None
    for r in range(GROUPS):
        for g in range(SETS):
            at = pl.ds(focal_start(m_ref[0], r, g), PW)
            for f in range(OWN):
                field = refs[r][f, g].astype(F32)
                for c in range(2):
                    value = field[c * PW : (c + 1) * PW]
                    if use_direct:
                        value = value + d_ref[f, c, at, :]
                    o_ref[f, c, at, :] = value


def finish(me, field, direct=None):
    use_direct = direct is not None
    return pl.pallas_call(
        functools.partial(finish_kernel, use_direct),
        in_specs=[pl.BlockSpec(memory_space=pltpu.SMEM)] + vmem(use_direct + GROUPS),
        out_specs=vmem()[0],
        out_shape=jax.ShapeDtypeStruct((OWN, 2, FOCAL, TILE), F32),
        compiler_params=params(),
        cost_estimate=pl.CostEstimate(flops=1_000_000, bytes_accessed=1_000_000, transcendentals=0),
        name="finish",
    )(me, *([direct] if use_direct else []), *field)


def split_bf16(table):
    high = table.astype(jnp.bfloat16.dtype)
    return np.stack([high, (table - high.astype(np.float64)).astype(jnp.bfloat16.dtype)])


def table_constants():
    turns = (np.arange(FREQS)[:, None] + LOWBIN) * np.arange(SAMPLES)[None, :] % SAMPLES
    angles = 2.0 * np.pi / SAMPLES * turns
    paired = np.stack([np.cos(angles), -np.sin(angles)], axis=1)
    spread = np.repeat(paired.reshape(GROUPS, OWN, 2, 1, SAMPLES), PW, axis=3)
    order = [3, 2, 1, 0, 3, 2, 1]
    rows = spread[order].reshape(len(order) * OWN * 2 * PW, SAMPLES)
    return split_bf16(np.ascontiguousarray(rows.T)), split_bf16(2.0 / SAMPLES * rows)


def own_tables(me):
    inverse, forward = table_constants()
    count = FREQS * 2 * PW
    start = (GROUPS - 1 - me) * (OWN * 2 * PW)
    return (
        lax.dynamic_slice_in_dim(jnp.asarray(inverse), start, count, 2),
        lax.dynamic_slice_in_dim(jnp.asarray(forward), start, count, 1),
    )


def exchange(parts):
    steps = [
        lax.ppermute(parts[r], "freq", [(i, (i + r) % GROUPS) for i in range(GROUPS)])
        for r in range(1, GROUPS)
    ]
    return [parts[0]] + steps


def own_onsets(onsets, me):
    return lax.dynamic_slice_in_dim(onsets, me * (SETS * PW), SETS * PW, 0)


def route(z):
    return lax.all_to_all(
        z.reshape(TILES, OWN * RMAX, 2 * FOCAL), "tile", 0, 0, tiled=True
    ).reshape(z.shape)


def per_device(direct_field, u_factors, v_factors, tile_ranks, onsets_source, onsets_receiver):
    me = lax.axis_index("freq")
    index = me.reshape(1).astype(jnp.int32)
    rank = tile_ranks[:, 0, :, None, None]
    mask = (lax.broadcasted_iota(jnp.int32, (1, 1, RMAX, 2 * FOCAL), 2) < rank).astype(BF)
    index, mask = lax.optimization_barrier((index, mask))

    plus = ()
    for _ in range(ITERS):
        z = project(True, index, direct_field, v_factors, plus)
        image = expand(True, route(z), u_factors, mask)
        if not plus:
            image, me = lax.optimization_barrier((image, me))
            tables = own_tables(me)
            sources, receivers = own_onsets(onsets_source, me), own_onsets(onsets_receiver, me)
        image = exchange(image)
        minus = exchange(window(image, sources, tables))
        w = project(False, index, mask, u_factors, minus)
        image = exchange(expand(False, route(w), v_factors))
        plus = exchange(window(image, receivers, tables))
    return (finish(index, plus, direct_field), finish(index, minus))


def solution(mesh):
    return jax.shard_map(
        per_device,
        mesh=mesh,
        in_specs=(
            P("freq", None, None, "tile"),
            P("freq", "tile", None, None, None, None),
            P("freq", None, "tile", None, None, None),
            P("freq", "tile", None),
            P(None, "tile"),
            P(None, "tile"),
        ),
        out_specs=(P("freq", None, None, "tile"), P("freq", None, None, "tile")),
        check_vma=False,
    )
```

```python
import functools

import numpy as np
import jax
import jax.numpy as jnp
from jax import lax
from jax.experimental import pallas as pl
from jax.experimental.pallas import tpu as pltpu
from jax.sharding import PartitionSpec as P

TILE = 256
RMAX = 16
FOCAL = 64
SAMPLES = 256
LOWBIN = 4
ITERS = 2
TILES = 64
FREQS = 16
GROUPS = 4
OWN = FREQS // GROUPS
PW = 8
SETS = FOCAL // GROUPS // PW
VMEM_LIMIT = 24 * 1024 * 1024
BF = jnp.bfloat16
F32 = jnp.float32

FIELD = (OWN, SETS, 2 * PW, TILE)


def params():
    return pltpu.CompilerParams(vmem_limit_bytes=VMEM_LIMIT)


def dot_nt(a, b):
    return lax.dot_general(a, b, (((1,), (1,)), ((), ())), preferred_element_type=F32)


def dot_tn(a, b):
    return lax.dot_general(a, b, (((0,), (0,)), ((), ())), preferred_element_type=F32)


def focal_start(m, r, g):
    return pl.multiple_of(((m + GROUPS - r) % GROUPS * SETS + g) * PW, PW)


def project_kernel(forward, use_field, m_ref, *refs):
    d_ref, f_ref, *refs, o_ref = refs
    for f in range(OWN):
        plain, turned = [], []
        for r in range(GROUPS):
            for g in range(SETS):
                real = imag = None
                if forward:
                    at = pl.ds(focal_start(m_ref[0], r, g), PW)
                    real, imag = d_ref[f, 0, at, :], d_ref[f, 1, at, :]
                if use_field:
                    field = refs[r][f, g].astype(F32)
                    real = field[:PW] if real is None else real + field[:PW]
                    imag = field[PW:] if imag is None else imag + field[PW:]
                plain += [real, imag]
                turned += [imag, -real]
        total = None
        for part, rows in enumerate((plain, turned)):
            x = jnp.concatenate(rows, axis=0).astype(BF)
            factor = f_ref[f, :, 0, part] if forward else f_ref[f, 0, :, part]
            term = dot_nt(factor.reshape(TILES * RMAX, TILE), x)
            total = term if total is None else total + term
        z = total.astype(BF).reshape(TILES, RMAX, 2 * FOCAL)
        o_ref[:, f] = z if forward else z * d_ref[f]


def vmem(count=1):
    return [pl.BlockSpec(memory_space=pltpu.VMEM)] * count


def project(forward, me, other, factors, field=()):
    return pl.pallas_call(
        functools.partial(project_kernel, forward, len(field) > 0),
        in_specs=[pl.BlockSpec(memory_space=pltpu.SMEM)] + vmem(2 + len(field)),
        out_specs=vmem()[0],
        out_shape=jax.ShapeDtypeStruct((TILES, OWN, RMAX, 2 * FOCAL), BF),
        compiler_params=params(),
        cost_estimate=pl.CostEstimate(flops=600_000_000, bytes_accessed=5_000_000, transcendentals=0),
        name="project",
    )(me, other, factors, *field)


def expand_kernel(forward, z_ref, f_ref, *outs):
    if forward:
        mask_ref, *outs = outs
    for f in range(OWN):
        z = z_ref[:, f] * mask_ref[f] if forward else z_ref[:, f]
        z = z.reshape(TILES * RMAX, 2 * FOCAL)
        straight, crossed = [
            dot_tn(z, (f_ref[f, 0, :, c] if forward else f_ref[f, :, 0, c]).reshape(TILES * RMAX, TILE))
            for c in range(2)
        ]
        for r in range(GROUPS):
            for g in range(SETS):
                at = (r * SETS + g) * 2 * PW
                real_part = straight[at : at + PW] - crossed[at + PW : at + 2 * PW]
                imag_part = straight[at + PW : at + 2 * PW] + crossed[at : at + PW]
                outs[-r % GROUPS][f, g] = jnp.concatenate([real_part, imag_part], axis=0).astype(BF)


def expand(forward, z, factors, mask=None):
    ins = [z, factors] + ([mask] if forward else [])
    return pl.pallas_call(
        functools.partial(expand_kernel, forward),
        in_specs=vmem(len(ins)),
        out_specs=vmem(GROUPS),
        out_shape=[jax.ShapeDtypeStruct(FIELD, BF)] * GROUPS,
        compiler_params=params(),
        cost_estimate=pl.CostEstimate(flops=600_000_000, bytes_accessed=5_000_000, transcendentals=0),
        name="expand",
    )(*ins)


def window_kernel(s0, s1, s2, s3, onset_ref, t_ref, f_ref, *outs):
    half = PW // 2
    rows = OWN * 2 * PW
    count = GROUPS * rows
    lane = lax.broadcasted_iota(jnp.int32, (1, count), 1) % half
    row = lax.broadcasted_iota(jnp.int32, (count, 1), 0) % half
    first = lax.broadcasted_iota(jnp.int32, (count, TILE), 0) % PW < half
    moment = lax.broadcasted_iota(jnp.int32, (SAMPLES, TILE), 0)

    def one(flags):
        return flags.astype(F32).astype(BF)

    lanes = [one(lane == p) for p in range(half)]
    rows_of = [one(row == p) for p in range(half)]
    inverse = [jnp.concatenate([t_ref[part] * pick for pick in lanes], axis=0) for part in range(2)]
    forward = [jnp.concatenate([f_ref[part] * pick for pick in rows_of], axis=1) for part in range(2)]
    for g in range(SETS):
        whole = jnp.concatenate(
            [ref[:, g].reshape(rows, TILE) for ref in (s0, s1, s2, s3)], axis=0
        ).astype(F32)
        down = pltpu.roll(whole, half, 0)
        up = pltpu.roll(whole, count - half, 0)
        fields = [jnp.where(first, whole, down).astype(BF), jnp.where(first, up, whole).astype(BF)]
        totals = []
        for part in range(2):
            trace = jnp.dot(inverse[part], fields[part], preferred_element_type=F32)
            kept = []
            for p in range(half):
                at = g * PW + part * half + p
                piece = trace[p * SAMPLES : (p + 1) * SAMPLES]
                kept.append(jnp.where(moment < onset_ref[at : at + 1, :], piece, 0.0).astype(BF))
            totals.append(
                jnp.dot(forward[part], jnp.concatenate(kept, axis=0), preferred_element_type=F32)
            )
        early, late = totals
        result = jnp.where(
            first, early + pltpu.roll(early, count - half, 0), late + pltpu.roll(late, half, 0)
        ).astype(BF)
        for r in range(GROUPS):
            outs[-r % GROUPS][:, g] = result[r * rows : (r + 1) * rows].reshape(OWN, 2 * PW, TILE)


def window(field, onset, tables):
    return pl.pallas_call(
        window_kernel,
        in_specs=vmem(GROUPS + 3),
        out_specs=vmem(GROUPS),
        out_shape=[jax.ShapeDtypeStruct(FIELD, BF)] * GROUPS,
        compiler_params=params(),
        cost_estimate=pl.CostEstimate(flops=1_100_000_000, bytes_accessed=1_000_000, transcendentals=0),
        name="window",
    )(*field, onset, *tables)


def finish_kernel(use_direct, *refs):
    refs = list(refs)
    o_ref = refs.pop()
    m_ref = refs.pop(0)
    d_ref = refs.pop(0) if use_direct else None
    for r in range(GROUPS):
        for g in range(SETS):
            at = pl.ds(focal_start(m_ref[0], r, g), PW)
            for f in range(OWN):
                field = refs[r][f, g].astype(F32)
                for c in range(2):
                    value = field[c * PW : (c + 1) * PW]
                    if use_direct:
                        value = value + d_ref[f, c, at, :]
                    o_ref[f, c, at, :] = value


def finish(me, field, direct=None):
    use_direct = direct is not None
    return pl.pallas_call(
        functools.partial(finish_kernel, use_direct),
        in_specs=[pl.BlockSpec(memory_space=pltpu.SMEM)] + vmem(use_direct + GROUPS),
        out_specs=vmem()[0],
        out_shape=jax.ShapeDtypeStruct((OWN, 2, FOCAL, TILE), F32),
        compiler_params=params(),
        cost_estimate=pl.CostEstimate(flops=1_000_000, bytes_accessed=1_000_000, transcendentals=0),
        name="finish",
    )(me, *([direct] if use_direct else []), *field)


def split_bf16(table):
    high = table.astype(jnp.bfloat16.dtype)
    return np.stack([high, (table - high.astype(np.float64)).astype(jnp.bfloat16.dtype)])


def table_constants():
    turns = (np.arange(FREQS)[:, None] + LOWBIN) * np.arange(SAMPLES)[None, :] % SAMPLES
    angles = 2.0 * np.pi / SAMPLES * turns
    paired = np.stack([np.cos(angles), -np.sin(angles)], axis=1)
    spread = np.repeat(paired.reshape(GROUPS, OWN, 2, 1, SAMPLES), PW, axis=3)
    order = [3, 2, 1, 0, 3, 2, 1]
    rows = spread[order].reshape(len(order) * OWN * 2 * PW, SAMPLES)
    early = (np.arange(rows.shape[0]) % PW < PW // 2)[:, None]

    def halves(table):
        high, low = split_bf16(table)
        return np.stack([np.where(early, high, low), np.where(early, low, high)])

    return np.ascontiguousarray(halves(rows).transpose(0, 2, 1)), halves(2.0 / SAMPLES * rows)


def own_tables(me):
    inverse, forward = table_constants()
    count = FREQS * 2 * PW
    start = (GROUPS - 1 - me) * (OWN * 2 * PW)
    return (
        lax.dynamic_slice_in_dim(jnp.asarray(inverse), start, count, 2),
        lax.dynamic_slice_in_dim(jnp.asarray(forward), start, count, 1),
    )


def exchange(parts):
    steps = [
        lax.ppermute(parts[r], "freq", [(i, (i + r) % GROUPS) for i in range(GROUPS)])
        for r in range(1, GROUPS)
    ]
    return [parts[0]] + steps


def own_onsets(onsets, me):
    return lax.dynamic_slice_in_dim(onsets, me * (SETS * PW), SETS * PW, 0)


def route(z):
    return lax.all_to_all(
        z.reshape(TILES, OWN * RMAX, 2 * FOCAL), "tile", 0, 0, tiled=True
    ).reshape(z.shape)


def per_device(direct_field, u_factors, v_factors, tile_ranks, onsets_source, onsets_receiver):
    me = lax.axis_index("freq")
    index = me.reshape(1).astype(jnp.int32)
    rank = tile_ranks[:, 0, :, None, None]
    mask = (lax.broadcasted_iota(jnp.int32, (1, 1, RMAX, 2 * FOCAL), 2) < rank).astype(BF)
    index, mask = lax.optimization_barrier((index, mask))

    plus = ()
    for _ in range(ITERS):
        z = project(True, index, direct_field, v_factors, plus)
        image = expand(True, route(z), u_factors, mask)
        if not plus:
            image, me = lax.optimization_barrier((image, me))
            tables = own_tables(me)
            sources, receivers = own_onsets(onsets_source, me), own_onsets(onsets_receiver, me)
        image = exchange(image)
        minus = exchange(window(image, sources, tables))
        w = project(False, index, mask, u_factors, minus)
        image = exchange(expand(False, route(w), v_factors))
        plus = exchange(window(image, receivers, tables))
    return (finish(index, plus, direct_field), finish(index, minus))


def solution(mesh):
    return jax.shard_map(
        per_device,
        mesh=mesh,
        in_specs=(
            P("freq", None, None, "tile"),
            P("freq", "tile", None, None, None, None),
            P("freq", None, "tile", None, None, None),
            P("freq", "tile", None),
            P(None, "tile"),
            P(None, "tile"),
        ),
        out_specs=(P("freq", None, None, "tile"), P("freq", None, None, "tile")),
        check_vma=False,
    )
```

```python
import functools

import numpy as np
import jax
import jax.numpy as jnp
from jax import lax
from jax.experimental import pallas as pl
from jax.experimental.pallas import tpu as pltpu
from jax.sharding import PartitionSpec as P

TILE = 256
RMAX = 16
FOCAL = 64
SAMPLES = 256
LOWBIN = 4
ITERS = 2
TILES = 64
FREQS = 16
GROUPS = 4
OWN = FREQS // GROUPS
PW = 8
SETS = FOCAL // GROUPS // PW
VMEM_LIMIT = 24 * 1024 * 1024
BF = jnp.bfloat16
F32 = jnp.float32

FIELD = (OWN, SETS, 2 * PW, TILE)


def params():
    return pltpu.CompilerParams(vmem_limit_bytes=VMEM_LIMIT)


def dot_nt(a, b):
    return lax.dot_general(a, b, (((1,), (1,)), ((), ())), preferred_element_type=F32)


def dot_tn(a, b):
    return lax.dot_general(a, b, (((0,), (0,)), ((), ())), preferred_element_type=F32)


def focal_start(m, r, g):
    return pl.multiple_of(((m + GROUPS - r) % GROUPS * SETS + g) * PW, PW)


def project_kernel(forward, use_field, m_ref, *refs):
    d_ref, f_ref, *refs, o_ref = refs
    for f in range(OWN):
        plain, turned = [], []
        for r in range(GROUPS):
            for g in range(SETS):
                real = imag = None
                if forward:
                    at = pl.ds(focal_start(m_ref[0], r, g), PW)
                    real, imag = d_ref[f, 0, at, :], d_ref[f, 1, at, :]
                if use_field:
                    field = refs[r][f, g].astype(F32)
                    real = field[:PW] if real is None else real + field[:PW]
                    imag = field[PW:] if imag is None else imag + field[PW:]
                plain += [real, imag]
                turned += [imag, -real]
        total = None
        for part, rows in enumerate((plain, turned)):
            x = jnp.concatenate(rows, axis=0).astype(BF)
            factor = f_ref[f, :, 0, part] if forward else f_ref[f, 0, :, part]
            term = dot_nt(factor.reshape(TILES * RMAX, TILE), x)
            total = term if total is None else total + term
        z = total.astype(BF).reshape(TILES, RMAX, 2 * FOCAL)
        o_ref[:, f] = z if forward else z * d_ref[f]


def vmem(count=1):
    return [pl.BlockSpec(memory_space=pltpu.VMEM)] * count


def project(forward, me, other, factors, field=()):
    return pl.pallas_call(
        functools.partial(project_kernel, forward, len(field) > 0),
        in_specs=[pl.BlockSpec(memory_space=pltpu.SMEM)] + vmem(2 + len(field)),
        out_specs=vmem()[0],
        out_shape=jax.ShapeDtypeStruct((TILES, OWN, RMAX, 2 * FOCAL), BF),
        compiler_params=params(),
        cost_estimate=pl.CostEstimate(flops=600_000_000, bytes_accessed=5_000_000, transcendentals=0),
        name="project",
    )(me, other, factors, *field)


def expand_kernel(forward, z_ref, f_ref, *outs):
    if forward:
        mask_ref, *outs = outs
    for f in range(OWN):
        z = z_ref[:, f] * mask_ref[f] if forward else z_ref[:, f]
        z = z.reshape(TILES * RMAX, 2 * FOCAL)
        sides = [
            (f_ref[f, 0, :, c] if forward else f_ref[f, :, 0, c]).reshape(TILES * RMAX, TILE)
            for c in range(2)
        ]
        both = dot_tn(z, jnp.concatenate(sides, axis=1))
        straight, crossed = both[:, :TILE], both[:, TILE:]
        for r in range(GROUPS):
            for g in range(SETS):
                at = (r * SETS + g) * 2 * PW
                real_part = straight[at : at + PW] - crossed[at + PW : at + 2 * PW]
                imag_part = straight[at + PW : at + 2 * PW] + crossed[at : at + PW]
                outs[-r % GROUPS][f, g] = jnp.concatenate([real_part, imag_part], axis=0).astype(BF)


def expand(forward, z, factors, mask=None):
    ins = [z, factors] + ([mask] if forward else [])
    return pl.pallas_call(
        functools.partial(expand_kernel, forward),
        in_specs=vmem(len(ins)),
        out_specs=vmem(GROUPS),
        out_shape=[jax.ShapeDtypeStruct(FIELD, BF)] * GROUPS,
        compiler_params=params(),
        cost_estimate=pl.CostEstimate(flops=600_000_000, bytes_accessed=5_000_000, transcendentals=0),
        name="expand",
    )(*ins)


def window_kernel(s0, s1, s2, s3, onset_ref, t_ref, f_ref, *outs):
    half = PW // 2
    rows = OWN * 2 * PW
    count = GROUPS * rows
    lane = lax.broadcasted_iota(jnp.int32, (1, count), 1) % half
    row = lax.broadcasted_iota(jnp.int32, (count, 1), 0) % half
    first = lax.broadcasted_iota(jnp.int32, (count, TILE), 0) % PW < half
    moment = lax.broadcasted_iota(jnp.int32, (SAMPLES, TILE), 0)

    def one(flags):
        return flags.astype(F32).astype(BF)

    lanes = [one(lane == p) for p in range(half)]
    rows_of = [one(row == p) for p in range(half)]
    inverse = [jnp.concatenate([t_ref[part] * pick for pick in lanes], axis=0) for part in range(2)]
    forward = [jnp.concatenate([f_ref[part] * pick for pick in rows_of], axis=1) for part in range(2)]
    for g in range(SETS):
        whole = jnp.concatenate(
            [ref[:, g].reshape(rows, TILE) for ref in (s0, s1, s2, s3)], axis=0
        ).astype(F32)
        down = pltpu.roll(whole, half, 0)
        up = pltpu.roll(whole, count - half, 0)
        fields = [jnp.where(first, whole, down).astype(BF), jnp.where(first, up, whole).astype(BF)]
        totals = []
        for part in range(2):
            trace = jnp.dot(inverse[part], fields[part], preferred_element_type=F32)
            kept = []
            for p in range(half):
                at = g * PW + part * half + p
                piece = trace[p * SAMPLES : (p + 1) * SAMPLES]
                kept.append(jnp.where(moment < onset_ref[at : at + 1, :], piece, 0.0).astype(BF))
            totals.append(
                jnp.dot(forward[part], jnp.concatenate(kept, axis=0), preferred_element_type=F32)
            )
        early, late = totals
        result = jnp.where(
            first, early + pltpu.roll(early, count - half, 0), late + pltpu.roll(late, half, 0)
        ).astype(BF)
        for r in range(GROUPS):
            outs[-r % GROUPS][:, g] = result[r * rows : (r + 1) * rows].reshape(OWN, 2 * PW, TILE)


def window(field, onset, tables):
    return pl.pallas_call(
        window_kernel,
        in_specs=vmem(GROUPS + 3),
        out_specs=vmem(GROUPS),
        out_shape=[jax.ShapeDtypeStruct(FIELD, BF)] * GROUPS,
        compiler_params=params(),
        cost_estimate=pl.CostEstimate(flops=1_100_000_000, bytes_accessed=1_000_000, transcendentals=0),
        name="window",
    )(*field, onset, *tables)


def finish_kernel(use_direct, *refs):
    refs = list(refs)
    o_ref = refs.pop()
    m_ref = refs.pop(0)
    d_ref = refs.pop(0) if use_direct else None
    for r in range(GROUPS):
        for g in range(SETS):
            at = pl.ds(focal_start(m_ref[0], r, g), PW)
            for f in range(OWN):
                field = refs[r][f, g].astype(F32)
                for c in range(2):
                    value = field[c * PW : (c + 1) * PW]
                    if use_direct:
                        value = value + d_ref[f, c, at, :]
                    o_ref[f, c, at, :] = value


def finish(me, field, direct=None):
    use_direct = direct is not None
    return pl.pallas_call(
        functools.partial(finish_kernel, use_direct),
        in_specs=[pl.BlockSpec(memory_space=pltpu.SMEM)] + vmem(use_direct + GROUPS),
        out_specs=vmem()[0],
        out_shape=jax.ShapeDtypeStruct((OWN, 2, FOCAL, TILE), F32),
        compiler_params=params(),
        cost_estimate=pl.CostEstimate(flops=1_000_000, bytes_accessed=1_000_000, transcendentals=0),
        name="finish",
    )(me, *([direct] if use_direct else []), *field)


def split_bf16(table):
    high = table.astype(jnp.bfloat16.dtype)
    return np.stack([high, (table - high.astype(np.float64)).astype(jnp.bfloat16.dtype)])


def table_constants():
    turns = (np.arange(FREQS)[:, None] + LOWBIN) * np.arange(SAMPLES)[None, :] % SAMPLES
    angles = 2.0 * np.pi / SAMPLES * turns
    paired = np.stack([np.cos(angles), -np.sin(angles)], axis=1)
    spread = np.repeat(paired.reshape(GROUPS, OWN, 2, 1, SAMPLES), PW, axis=3)
    order = [3, 2, 1, 0, 3, 2, 1]
    rows = spread[order].reshape(len(order) * OWN * 2 * PW, SAMPLES)
    early = (np.arange(rows.shape[0]) % PW < PW // 2)[:, None]

    def halves(table):
        high, low = split_bf16(table)
        return np.stack([np.where(early, high, low), np.where(early, low, high)])

    return np.ascontiguousarray(halves(rows).transpose(0, 2, 1)), halves(2.0 / SAMPLES * rows)


def own_tables(me):
    inverse, forward = table_constants()
    count = FREQS * 2 * PW
    start = (GROUPS - 1 - me) * (OWN * 2 * PW)
    return (
        lax.dynamic_slice_in_dim(jnp.asarray(inverse), start, count, 2),
        lax.dynamic_slice_in_dim(jnp.asarray(forward), start, count, 1),
    )


def exchange(parts):
    steps = [
        lax.ppermute(parts[r], "freq", [(i, (i + r) % GROUPS) for i in range(GROUPS)])
        for r in range(1, GROUPS)
    ]
    return [parts[0]] + steps


def own_onsets(onsets, me):
    return lax.dynamic_slice_in_dim(onsets, me * (SETS * PW), SETS * PW, 0)


def route(z):
    return lax.all_to_all(
        z.reshape(TILES, OWN * RMAX, 2 * FOCAL), "tile", 0, 0, tiled=True
    ).reshape(z.shape)


def per_device(direct_field, u_factors, v_factors, tile_ranks, onsets_source, onsets_receiver):
    me = lax.axis_index("freq")
    index = me.reshape(1).astype(jnp.int32)
    rank = tile_ranks[:, 0, :, None, None]
    mask = (lax.broadcasted_iota(jnp.int32, (1, 1, RMAX, 2 * FOCAL), 2) < rank).astype(BF)
    index, mask = lax.optimization_barrier((index, mask))

    plus = ()
    for _ in range(ITERS):
        z = project(True, index, direct_field, v_factors, plus)
        image = expand(True, route(z), u_factors, mask)
        if not plus:
            image, me = lax.optimization_barrier((image, me))
            tables = own_tables(me)
            sources, receivers = own_onsets(onsets_source, me), own_onsets(onsets_receiver, me)
        image = exchange(image)
        minus = exchange(window(image, sources, tables))
        w = project(False, index, mask, u_factors, minus)
        image = exchange(expand(False, route(w), v_factors))
        plus = exchange(window(image, receivers, tables))
    return (finish(index, plus, direct_field), finish(index, minus))


def solution(mesh):
    return jax.shard_map(
        per_device,
        mesh=mesh,
        in_specs=(
            P("freq", None, None, "tile"),
            P("freq", "tile", None, None, None, None),
            P("freq", None, "tile", None, None, None),
            P("freq", "tile", None),
            P(None, "tile"),
            P(None, "tile"),
        ),
        out_specs=(P("freq", None, None, "tile"), P("freq", None, None, "tile")),
        check_vma=False,
    )
```
